512 devices in a mesh: dp: 32 (over x, z_lo), tensor: 16 (over y, z_hi, core).
Axes of the slice: x: 4, y: 4, z: 16 (z_hi: 2, z_lo: 8; z = z_hi * 8 + z_lo), core: 2. Of those that a mesh axis runs over, the one named last changes fastest.
Arguments:
- tokens: bfloat16 [8192, 2048], P(('dp', 'tensor')), may hold values from -24 to 24
- masked: int32 [8192], P(('dp', 'tensor')), may hold values 0 or 1
- mask_vector: bfloat16 [2048], replicated, may hold values from -4 to 4
- gate_weight: bfloat16 [2048, 6144], P(None, 'tensor'), may hold values from -0.125 to 0.125
- up_weight: bfloat16 [2048, 6144], P(None, 'tensor'), may hold values from -0.125 to 0.125
- cotangent: bfloat16 [8192, 6144], P('dp', 'tensor'), may hold values from -6 to 6
Outputs:
- hidden: bfloat16 [8192, 6144], P('dp', 'tensor')
- token_grad: bfloat16 [8192, 2048], P(('dp', 'tensor'))
- gate_grad: float32 [2048, 6144], P('dp', 'tensor')
- up_grad: float32 [2048, 6144], P('dp', 'tensor')
The draws below stay inside these ranges and needn't reach their ends.
All inputs are finite; a program needn't handle non-finite values. No bound on the sum of `masked` on one device may be relied on, other than what follows from the above.
Results may differ from the reference program's by a relative error of at most 0.029.
Values may be sent and summed in bfloat16 or wider, within the bound.
No kernel may reach another device: no remote copies, remote signals or barrier semaphores. Data moves between devices by JAX's collectives and lax.ppermute only.
A program may use at most 64 MiB of HBM per device.

```python
import jax
import jax.numpy as jnp
from jax import lax

D = 2048
FF = 6144
GROUP = 256
TOKENS = 8192
N_DP = 32
N_TENSOR = 16


def with_ends(entries, rng, smallest, largest):
    index_at = [jax.random.randint(jax.random.fold_in(rng, axis), (), 0, length) for axis, length in enumerate(entries.shape)]
    longest = entries.shape.index(max(entries.shape))
    next_to = index_at[:longest] + [(index_at[longest] + 1) % entries.shape[longest]] + index_at[longest + 1:]
    return entries.at[tuple(index_at)].set(smallest).at[tuple(next_to)].set(largest)


def with_spikes(values, stream_key, source, target, parts, factor):
    owner, partner = [(jnp.arange(values.shape[axis_at]) // (values.shape[axis_at] // parts)).reshape([-1 if axis == axis_at else 1 for axis in range(values.ndim)]) for axis_at in (source, target)]
    chosen = jax.random.permutation(stream_key, parts)[partner]
    strong = (owner == chosen) | (owner == (partner + parts // 2) % parts)
    return jnp.where(strong, factor * values, values)


def level_of(own_key, shape, split, least, largest):
    def one(axis_at, parts):
        draws = jax.random.uniform(jax.random.fold_in(jax.random.fold_in(own_key, 6), axis_at), (parts,), jnp.float32, least / len(split), largest / len(split))
        return jnp.repeat(jnp.exp(draws), shape[axis_at] // parts).reshape((-1,) + (1,) * (len(shape) - axis_at - 1))

    loudness = one(*split[0])
    for cut in split[1:]:
        loudness = loudness * one(*cut)
    return loudness


def normal_values(key, dims, deviation, reach, shards=(), kind=jnp.bfloat16):
    loudness = level_of(key, dims, shards, -0.22, 0.18) if shards else 1.0
    values = jax.random.normal(key, dims, jnp.float32) * deviation * loudness
    return jnp.minimum(jnp.maximum(values, -reach), reach).astype(kind)


def bell_draw_with(rng, dims, deviation, limit, shards, heavy, kind=jnp.bfloat16):
    array = deviation * jax.random.normal(rng, dims, jnp.float32)
    if shards:
        array = array * level_of(rng, dims, shards, -0.22, 0.18)
    return jnp.clip(with_spikes(array, jax.random.fold_in(rng, 3), *heavy), -limit, limit).astype(kind)


def setup_inputs(seed: int = 0) -> dict:
    seeds = jax.random.split(jax.random.key(seed), 7)
    tokens = bell_draw_with(seeds[0], (TOKENS, D), 1.0, 24.0, ((0, 512),), (0, 1, 512, 6.0))
    masked = with_ends((jax.random.randint(seeds[1], (TOKENS,), 0, 4) < 1).astype(jnp.int32), jax.random.fold_in(seeds[1], 1), 0, 1)
    mask_vector = normal_values(seeds[2], (D,), 1.0, 4.0)
    gate_weight = normal_values(seeds[3], (D, FF), D ** -0.5, 0.125, ((1, 16),))
    up_weight = normal_values(seeds[4], (D, FF), D ** -0.5, 0.125, ((1, 16),))
    cotangent = bell_draw_with(seeds[5], (TOKENS, FF), 1.0, 6.0, ((0, 32), (1, 16)), (1, 0, 32, 2.75))
    return dict(tokens=tokens, masked=masked, mask_vector=mask_vector, gate_weight=gate_weight, up_weight=up_weight, cotangent=cotangent)


def reference(tokens, masked, mask_vector, gate_weight, up_weight, cotangent):
    flag = masked[:, None] == 1
    mixed_in = jnp.where(flag, mask_vector[None, :], tokens)
    mixed_f = mixed_in.astype(jnp.float32)
    inverse = lax.rsqrt(lax.optimization_barrier(jnp.mean(mixed_f * mixed_f, axis=-1, keepdims=True)) + 1e-06)
    normed_full = mixed_f * inverse
    normed = normed_full.astype(jnp.bfloat16)
    gate = jnp.dot(normed, gate_weight, preferred_element_type=jnp.float32)
    up = jnp.dot(normed, up_weight, preferred_element_type=jnp.float32)
    sig = jax.nn.sigmoid(gate)
    hidden = (gate * sig * up).astype(jnp.bfloat16)
    cot = cotangent.astype(jnp.float32)
    up_delta = (cot * gate * sig).astype(jnp.bfloat16)
    gate_delta = (cot * up * sig * (1.0 + gate * (1.0 - sig))).astype(jnp.bfloat16)
    width = FF // N_TENSOR

    def hidden_group(total, index):
        start = (index * width).astype(jnp.int32)
        gd = lax.dynamic_slice_in_dim(gate_delta, start, width, 1)
        ud = lax.dynamic_slice_in_dim(up_delta, start, width, 1)
        gw = lax.dynamic_slice_in_dim(gate_weight, start, width, 1)
        uw = lax.dynamic_slice_in_dim(up_weight, start, width, 1)
        part = jnp.dot(gd, gw.T, preferred_element_type=jnp.float32) + jnp.dot(ud, uw.T, preferred_element_type=jnp.float32)
        part = part.astype(jnp.bfloat16).astype(jnp.float32)
        return (total + part, None)
    normed_grad, _ = lax.scan(hidden_group, jnp.zeros((TOKENS, D), jnp.float32), jnp.arange(N_TENSOR, dtype=jnp.int32))
    inner = lax.optimization_barrier(jnp.mean(normed_grad * normed_full, axis=-1, keepdims=True))
    token_grad = jnp.where(flag, 0.0, inverse * (normed_grad - normed_full * inner)).astype(jnp.bfloat16)

    def row_block(totals, index):
        start = (index * GROUP).astype(jnp.int32)
        nb = lax.dynamic_slice_in_dim(normed, start, GROUP, 0)
        gd = lax.dynamic_slice_in_dim(gate_delta, start, GROUP, 0)
        ud = lax.dynamic_slice_in_dim(up_delta, start, GROUP, 0)
        gpart = jnp.dot(nb.T, gd, preferred_element_type=jnp.float32).astype(jnp.bfloat16).astype(jnp.float32)
        upart = jnp.dot(nb.T, ud, preferred_element_type=jnp.float32).astype(jnp.bfloat16).astype(jnp.float32)
        return ((totals[0] + gpart, totals[1] + upart), None)
    zeros = jnp.zeros((D, FF), jnp.float32)
    grads, _ = lax.scan(row_block, (zeros, zeros), jnp.arange(N_DP, dtype=jnp.int32))
    return (hidden, token_grad, grads[0], grads[1])
```

```python
import jax
import jax.numpy as jnp
from jax import lax
from jax.sharding import PartitionSpec as P

NX, NZ = 4, 8
NY, NH, NC = 4, 2, 2
F32, BF16 = jnp.float32, jnp.bfloat16


def pick(array, index, axis):
    return lax.dynamic_index_in_dim(array, index, axis, keepdims=False)


def move(array, axis_name, count, target):
    return lax.ppermute(array, axis_name, [(i, target(i)) for i in range(count)])


def to_core(array):
    return move(array, "tensor", 16, lambda t: t ^ 1)


def to_high(array):
    return move(array, "tensor", 16, lambda t: t ^ 2)


def to_y(array, step):
    return move(array, "tensor", 16, lambda t: (t + 4 * step) % 16)


def to_x(array, step):
    return move(array, "dp", 32, lambda d: (d + 8 * step) % 32)


def to_z(array, bit):
    return move(array, "dp", 32, lambda d: d ^ bit)


def gather_rows(normed, y, high, core):
    rows, depth = normed.shape
    other = to_high(normed)
    pair = jnp.where(high == 0, jnp.stack([normed, other]), jnp.stack([other, normed]))
    got = [to_y(pair, step) for step in (1, 2, 3)]
    ring = jnp.stack([pair, got[2], got[1], got[0]])
    quad = lax.dynamic_slice_in_dim(jnp.concatenate([ring, ring]), (NY - y) % NY, NY, 0)
    far = to_core(quad)
    both = jnp.where(core == 0, jnp.stack([quad, far], axis=2), jnp.stack([far, quad], axis=2))
    return both.reshape(16 * rows, depth)


def scatter_rows(share, y, high, core):
    rows = share.shape[0] // 16
    share = share.reshape(NY, NH, NC, rows, -1)
    got = to_core(pick(share, 1 - core, 2))
    total = pick(share, core, 2).astype(F32) + got.astype(F32)
    sent = total.astype(BF16)
    got = [to_y(pick(sent, (y + step) % NY, 0), step) for step in (1, 2, 3)]
    total = pick(total, y, 0)
    for part in got:
        total = total + part.astype(F32)
    got = to_high(pick(total, 1 - high, 0).astype(BF16))
    return pick(total, high, 0) + got.astype(F32)


def scatter_weight(part, x, z):
    rows, width = part.shape
    rows = rows // (NX * NZ)
    part = part.reshape(NX, 2, NZ // 2, rows, width)
    far = pick(part, (x + 2) % NX, 0)
    from_left = to_x(far[0], 1)
    from_right = to_x(far[1], -1)
    right = pick(part, (x + 1) % NX, 0)
    left = pick(part, (x + 3) % NX, 0)
    low = (right[0].astype(F32) + from_left.astype(F32)).astype(BF16)
    high = (left[1].astype(F32) + from_right.astype(F32)).astype(BF16)
    from_left = to_x(jnp.stack([low, right[1]]), 1)
    from_right = to_x(jnp.stack([left[0], high]), -1)
    total = pick(part, x, 0).astype(F32) + from_left.astype(F32) + from_right.astype(F32)
    total = total.reshape(2, 2, 2, rows, width)
    bits = ((z // 4) % 2, (z // 2) % 2, z % 2)
    for axis, bit in ((2, 1), (1, 2), (0, 4)):
        got = to_z(pick(total, 1 - bits[axis], axis).astype(BF16), bit)
        total = pick(total, bits[axis], axis) + got.astype(F32)
    return total


def shards(tokens, masked, mask_vector, gate_weight, up_weight, cotangent):
    dp = lax.axis_index("dp")
    tensor = lax.axis_index("tensor")
    x, z = dp // NZ, dp % NZ
    y, high, core = tensor // 4, (tensor // 2) % 2, tensor % 2
    flag = masked[:, None] == 1
    mixed_in = jnp.where(flag, mask_vector[None, :], tokens)
    mixed_f = mixed_in.astype(F32)
    inverse = lax.rsqrt(jnp.mean(mixed_f * mixed_f, axis=-1, keepdims=True) + 1e-06)
    normed_full = mixed_f * inverse
    gathered = gather_rows(normed_full.astype(BF16), y, high, core)
    gate = jnp.dot(gathered, gate_weight, preferred_element_type=F32)
    up = jnp.dot(gathered, up_weight, preferred_element_type=F32)
    sig = jax.nn.sigmoid(gate)
    hidden = (gate * sig * up).astype(BF16)
    cot = cotangent.astype(F32)
    up_delta = (cot * gate * sig).astype(BF16)
    gate_delta = (cot * up * sig * (1.0 + gate * (1.0 - sig))).astype(BF16)
    contract_last = (((1,), (1,)), ((), ()))
    contract_first = (((0,), (0,)), ((), ()))
    first = lax.dot_general(gathered, gate_delta, contract_first, preferred_element_type=F32)
    second = lax.dot_general(gathered, up_delta, contract_first, preferred_element_type=F32)
    gate_grad = scatter_weight(first.astype(BF16), x, z)
    up_grad = scatter_weight(second.astype(BF16), x, z)
    first = lax.dot_general(gate_delta, gate_weight, contract_last, preferred_element_type=F32)
    second = lax.dot_general(up_delta, up_weight, contract_last, preferred_element_type=F32)
    normed_grad = scatter_rows((first + second).astype(BF16), y, high, core)
    inner = jnp.mean(normed_grad * normed_full, axis=-1, keepdims=True)
    token_grad = jnp.where(flag, 0.0, inverse * (normed_grad - normed_full * inner)).astype(BF16)
    return (hidden, token_grad, gate_grad, up_grad)


def solution(mesh):
    return jax.shard_map(
        shards,
        mesh=mesh,
        in_specs=(
            P(("dp", "tensor"), None),
            P(("dp", "tensor")),
            P(),
            P(None, "tensor"),
            P(None, "tensor"),
            P("dp", "tensor"),
        ),
        out_specs=(
            P("dp", "tensor"),
            P(("dp", "tensor"), None),
            P("dp", "tensor"),
            P("dp", "tensor"),
        ),
        check_vma=False,
    )
```

```python
import jax
import jax.numpy as jnp
from jax import lax
from jax.experimental import pallas as pl
from jax.experimental.pallas import tpu as pltpu
from jax.sharding import PartitionSpec as P

NX, NZ = 4, 8
NY, NH, NC = 4, 2, 2
F32, BF16 = jnp.float32, jnp.bfloat16


def pick(array, index, axis):
    return lax.dynamic_index_in_dim(array, index, axis, keepdims=False)


def move(array, axis_name, count, target):
    return lax.ppermute(array, axis_name, [(i, target(i)) for i in range(count)])


def to_core(array):
    return move(array, "tensor", 16, lambda t: t ^ 1)


def to_y(array, target):
    return move(array, "tensor", 16, lambda t: 4 * target(t // 4) + t % 4)


def to_x(array, step):
    return move(array, "dp", 32, lambda d: (d + 8 * step) % 32)


def to_z(array, bit):
    return move(array, "dp", 32, lambda d: d ^ bit)


def to_high(array):
    return move(array, "tensor", 16, lambda t: t ^ 2)


def copy_kernel(array_ref, other_ref, out_ref):
    out_ref[...] = array_ref[...]


def after(array, other):
    return pl.pallas_call(
        copy_kernel,
        out_shape=jax.ShapeDtypeStruct(array.shape, array.dtype),
        in_specs=[pl.BlockSpec(memory_space=pltpu.VMEM), pl.BlockSpec(memory_space=pl.ANY)],
        out_specs=pl.BlockSpec(memory_space=pltpu.VMEM),
    )(array, other)


def gather_rows(normed, y, high, core):
    rows, depth = normed.shape
    across = to_high(normed)
    other = to_y(normed, lambda i: 3 - i)
    two = jnp.where(y < 2, jnp.stack([normed, other]), jnp.stack([other, normed]))
    got = to_y(jnp.concatenate([two, across[None]]), lambda i: i ^ 1)
    outer, even = (y == 0) | (y == 3), y % 2 == 0
    ends, middle = jnp.where(outer, two, got[:2]), jnp.where(outer, got[:2], two)
    near = jnp.stack([ends[0], middle[0], middle[1], ends[1]])
    two = jnp.where(even, jnp.stack([across, got[2]]), jnp.stack([got[2], across]))
    other = to_y(two, lambda i: 3 - i)
    away = jnp.where(y < 2, jnp.concatenate([two, other]), jnp.concatenate([other, two]))
    quad = jnp.where(high == 0, jnp.stack([near, away], axis=1), jnp.stack([away, near], axis=1))
    far = to_core(quad)
    both = jnp.where(core == 0, jnp.stack([quad, far], axis=2), jnp.stack([far, quad], axis=2))
    return both.reshape(16 * rows, depth)


def scatter_rows(share, early, late, y, high, core):
    rows = share.shape[0] // 16
    share = share.reshape(NY, NH, NC, rows, -1)
    got = to_core(pick(share, 1 - core, 2))
    total = pick(share, core, 2).astype(F32) + got.astype(F32)
    outer = (y == 0) | (y == 3)
    ends, middle = jnp.stack([total[0], total[3]]), total[1:3]
    got = to_y(jnp.where(outer, middle, ends).astype(BF16), lambda i: i ^ 1)
    total = jnp.where(outer, ends, middle) + got.astype(F32)
    sent = after(jnp.where(y < 2, total[1], total[0]).astype(BF16), early)
    got = to_y(sent, lambda i: 3 - i)
    total = jnp.where(y < 2, total[0], total[1]) + got.astype(F32)
    got = to_high(pick(total, 1 - high, 0).astype(BF16))
    return pick(total, high, 0) + after(got, late).astype(F32)


LANES = 128


def call(kernel, outs, scratch, place, flops, *arrays):
    moved = sum(a.size * a.dtype.itemsize for a in (*arrays, *outs))
    return pl.pallas_call(
        kernel,
        out_shape=outs,
        in_specs=[pl.BlockSpec(memory_space=pltpu.SMEM)]
        + [pl.BlockSpec(memory_space=pltpu.VMEM)] * len(arrays),
        out_specs=[pl.BlockSpec(memory_space=pltpu.VMEM)] * len(outs),
        scratch_shapes=scratch,
        compiler_params=pltpu.CompilerParams(vmem_limit_bytes=32 * 2**20),
        cost_estimate=pl.CostEstimate(flops=flops, bytes_accessed=moved, transcendentals=0),
    )(place, *arrays)


def columns(ref, index, rows=slice(None)):
    width = ref.shape[1] // NX
    return ref[rows, pl.ds(pl.multiple_of(index * width, LANES), width)]


def put(ref, row, block):
    for start in range(0, block.shape[1], LANES):
        ref[row : row + block.shape[0], :] = block[:, start : start + LANES]
        row += block.shape[0]
    return row


def lanes(ref, row, rows, width):
    return jnp.concatenate([ref[row + i * rows : row + (i + 1) * rows, :] for i in range(width // LANES)], axis=1)


def pack_kernel(place, rows_ref, gate_ref, up_ref, right_ref, left_ref, gate_out, up_out):
    x, core = place[0], place[1]
    half = rows_ref.shape[0] // 2
    mine = pl.ds(pl.multiple_of(core * half, half), half)
    row = put(right_ref, 0, up_ref[...])
    row = put(right_ref, row, columns(rows_ref, lax.rem(x + 1, NX), mine))
    row = put(right_ref, row, gate_ref[...])
    put(right_ref, row, columns(rows_ref, lax.rem(x + 2, NX), slice(0, half)))
    row = put(left_ref, 0, gate_ref[...])
    row = put(left_ref, row, columns(rows_ref, lax.rem(x + 3, NX), mine))
    row = put(left_ref, row, up_ref[...])
    put(left_ref, row, columns(rows_ref, lax.rem(x + 2, NX), slice(half, 2 * half)))
    gate_out[...] = gate_ref[...]
    up_out[...] = up_ref[...]


def times(rows, deltas, out, total=None):
    depth = rows.shape[1]
    for start in range(0, depth, LANES):
        part = lax.dot_general(
            rows[:, start : start + LANES],
            deltas[...],
            (((0,), (0,)), ((), ())),
            preferred_element_type=F32,
        )
        if total is not None:
            part = part + total[start : start + LANES, :]
        out[start : start + LANES, :] = part


def near_kernel(place, rows_ref, gate_ref, up_ref, left_ref, right_ref, other_ref, out_ref, rows, deltas):
    x, core = place[0], place[1]
    count, width = gate_ref.shape
    half, quarter = count // 2, rows_ref.shape[1] // NX
    mine = pl.multiple_of(core * half, half)
    others = pl.multiple_of((1 - core) * half, half)
    chunk, piece = count * width // LANES, half * quarter // LANES
    rows[0:count, :] = columns(rows_ref, x)
    deltas[0:count, 0:width] = gate_ref[...]
    deltas[0:count, width : 2 * width] = up_ref[...]
    for step, ref in ((1, left_ref), (2, right_ref)):
        rows[pl.ds(step * count + mine, half), :] = lanes(ref, chunk, half, quarter)
        rows[pl.ds(step * count + others, half), :] = lanes(other_ref, (step - 1) * piece, half, quarter)
        low, high = lanes(ref, 0, count, width), lanes(ref, chunk + piece, count, width)
        gate, up = (high, low) if step == 1 else (low, high)
        deltas[step * count : (step + 1) * count, 0:width] = gate
        deltas[step * count : (step + 1) * count, width : 2 * width] = up
    times(rows, deltas, out_ref)


def far_kernel(
    place, near_ref, left_ref, right_ref, gate_out, up_out, gate_keep, up_keep, rows, deltas, total
):
    bit = place[2]
    count, width = rows.shape[0], gate_out.shape[1]
    half, quarter = count // 2, rows.shape[1]
    chunk = count * width // LANES
    rows[0:half, :] = lanes(left_ref, chunk, half, quarter)
    rows[half:count, :] = lanes(right_ref, chunk, half, quarter)
    deltas[:, 0:width] = lanes(left_ref, 0, count, width)
    deltas[:, width : 2 * width] = lanes(right_ref, 0, count, width)
    times(rows, deltas, total, near_ref)
    small = quarter // NZ
    for k in range(NZ // 2):
        to = slice(k * small, (k + 1) * small)
        keep = pl.ds(pl.multiple_of((2 * k + bit) * small, small), small)
        send = pl.ds(pl.multiple_of((2 * k + 1 - bit) * small, small), small)
        gate_keep[to, :] = total[keep, 0:width]
        up_keep[to, :] = total[keep, width : 2 * width]
        gate_out[to, :] = total[send, 0:width].astype(BF16)
        up_out[to, :] = total[send, width : 2 * width].astype(BF16)


def weight_parts(gathered, gate_delta, up_delta, x, z, core):
    count, width = gate_delta.shape
    half, quarter = count // 2, gathered.shape[1] // NX
    chunk, piece = count * width // LANES, half * quarter // LANES
    place = jnp.stack([x, core, z % 2]).astype(jnp.int32)
    shape = jax.ShapeDtypeStruct
    message = shape((2 * (chunk + piece), LANES), BF16)
    outs = [message] * 2 + [shape(gate_delta.shape, BF16)] * 2
    right, left, gate_delta, up_delta = call(
        pack_kernel, outs, [], place, 0, gathered, gate_delta, up_delta
    )
    left, right = to_x(right, 1), to_x(left, -1)
    far_left = to_x(left[chunk + piece :], 1)
    far_right = to_x(right[chunk + piece :], -1)
    near = slice(chunk, chunk + piece)
    other = to_core(jnp.concatenate([left[near], right[near]]))
    both = pltpu.VMEM((3 * count, quarter), BF16), pltpu.VMEM((3 * count, 2 * width), BF16)
    outs = [shape((quarter, 2 * width), F32)]
    flops = 2 * 3 * count * quarter * 2 * width
    (total,) = call(
        near_kernel, outs, both, place, flops, gathered, gate_delta, up_delta, left, right, other
    )
    both = pltpu.VMEM((count, quarter), BF16), pltpu.VMEM((count, 2 * width), BF16)
    outs = [shape((quarter // 2, width), BF16)] * 2 + [shape((quarter // 2, width), F32)] * 2
    scratch = [*both, pltpu.VMEM((quarter, 2 * width), F32)]
    parts = call(far_kernel, outs, scratch, place, flops // 3, total, far_left, far_right)
    return parts, gate_delta, up_delta, other


def scatter_z(sent, kept, z):
    total = kept + to_z(sent, 1).astype(F32)
    total = total.reshape(2, 2, total.shape[0] * 2 // NZ, -1)
    bits = ((z // 4) % 2, (z // 2) % 2)
    for axis, bit in ((1, 2), (0, 4)):
        sent = pick(total, 1 - bits[axis], axis).astype(BF16)
        got = to_z(sent, bit)
        total = pick(total, bits[axis], axis) + got.astype(F32)
    return total, sent


def shards(tokens, masked, mask_vector, gate_weight, up_weight, cotangent):
    dp = lax.axis_index("dp")
    tensor = lax.axis_index("tensor")
    x, z = dp // NZ, dp % NZ
    y, high, core = tensor // 4, (tensor // 2) % 2, tensor % 2
    flag = masked[:, None] == 1
    mixed_in = jnp.where(flag, mask_vector[None, :], tokens)
    mixed_f = mixed_in.astype(F32)
    inverse = lax.rsqrt(jnp.mean(mixed_f * mixed_f, axis=-1, keepdims=True) + 1e-06)
    normed_full = mixed_f * inverse
    gathered = gather_rows(normed_full.astype(BF16), y, high, core)
    gate = jnp.dot(gathered, gate_weight, preferred_element_type=F32)
    up = jnp.dot(gathered, up_weight, preferred_element_type=F32)
    sig = jax.nn.sigmoid(gate)
    hidden = (gate * sig * up).astype(BF16)
    cot = cotangent.astype(F32)
    up_delta = (cot * gate * sig).astype(BF16)
    gate_delta = (cot * up * sig * (1.0 + gate * (1.0 - sig))).astype(BF16)
    sent, gate_delta, up_delta, other = weight_parts(gathered, gate_delta, up_delta, x, z, core)
    gate_grad, late = scatter_z(sent[0], sent[2], z)
    up_grad, _ = scatter_z(sent[1], sent[3], z)
    contract_last = (((1,), (1,)), ((), ()))
    first = lax.dot_general(gate_delta, gate_weight, contract_last, preferred_element_type=F32)
    second = lax.dot_general(up_delta, up_weight, contract_last, preferred_element_type=F32)
    normed_grad = scatter_rows((first + second).astype(BF16), other, late, y, high, core)
    inner = jnp.mean(normed_grad * normed_full, axis=-1, keepdims=True)
    token_grad = jnp.where(flag, 0.0, inverse * (normed_grad - normed_full * inner)).astype(BF16)
    return (hidden, token_grad, gate_grad, up_grad)


def solution(mesh):
    return jax.shard_map(
        shards,
        mesh=mesh,
        in_specs=(
            P(("dp", "tensor"), None),
            P(("dp", "tensor")),
            P(),
            P(None, "tensor"),
            P(None, "tensor"),
            P("dp", "tensor"),
        ),
        out_specs=(
            P("dp", "tensor"),
            P(("dp", "tensor"), None),
            P("dp", "tensor"),
            P("dp", "tensor"),
        ),
        check_vma=False,
    )
```

```python
import jax
import jax.numpy as jnp
from jax import lax
from jax.experimental import pallas as pl
from jax.experimental.pallas import tpu as pltpu
from jax.sharding import PartitionSpec as P

NX, NZ = 4, 8
NY, NH, NC = 4, 2, 2
F32, BF16 = jnp.float32, jnp.bfloat16


def pick(array, index, axis):
    return lax.dynamic_index_in_dim(array, index, axis, keepdims=False)


def move(array, axis_name, count, target):
    return lax.ppermute(array, axis_name, [(i, target(i)) for i in range(count)])


def to_core(array):
    return move(array, "tensor", 16, lambda t: t ^ 1)


def to_y(array, target):
    return move(array, "tensor", 16, lambda t: 4 * target(t // 4) + t % 4)


def to_x(array, step):
    return move(array, "dp", 32, lambda d: (d + 8 * step) % 32)


def to_z(array, bit):
    return move(array, "dp", 32, lambda d: d ^ bit)


HIGH_PAIRS = [[t, t + 2] for t in range(16) if (t // 2) % 2 == 0]


def copy_kernel(array_ref, other_ref, out_ref):
    out_ref[...] = array_ref[...]


def after(array, other):
    return pl.pallas_call(
        copy_kernel,
        out_shape=jax.ShapeDtypeStruct(array.shape, array.dtype),
        in_specs=[pl.BlockSpec(memory_space=pltpu.VMEM), pl.BlockSpec(memory_space=pl.ANY)],
        out_specs=pl.BlockSpec(memory_space=pltpu.VMEM),
        compiler_params=pltpu.CompilerParams(vmem_limit_bytes=2 * 2**20),
    )(array, other)


def two_of_y(block, y):
    other = to_y(block, lambda i: 3 - i)
    return jnp.where(y < 2, jnp.stack([block, other]), jnp.stack([other, block]))


def all_of_y(two, y):
    other = to_y(two, lambda i: i ^ 1)
    outer = (y == 0) | (y == 3)
    ends, middle = jnp.where(outer, two, other), jnp.where(outer, other, two)
    return jnp.stack([ends[0], middle[0], middle[1], ends[1]])


def gather_rows(normed, y, high, core):
    rows, depth = normed.shape
    pair = lax.all_gather(normed, "tensor", axis=0, axis_index_groups=HIGH_PAIRS)
    two = two_of_y(normed, y)
    near = all_of_y(two, y)
    away = all_of_y(two_of_y(after(pick(pair, 1 - high, 0), near), y), y)
    quad = jnp.where(high == 0, jnp.stack([near, away], axis=1), jnp.stack([away, near], axis=1))
    far = to_core(quad)
    both = jnp.where(core == 0, jnp.stack([quad, far], axis=2), jnp.stack([far, quad], axis=2))
    return both.reshape(16 * rows, depth)


def scatter_rows(share, late, y, core):
    rows = share.shape[0] // 16
    share = share.reshape(NY, NH, NC, rows, -1)
    got = to_core(pick(share, 1 - core, 2))
    total = pick(share, core, 2).astype(F32) + got.astype(F32)
    outer = (y == 0) | (y == 3)
    ends, middle = jnp.stack([total[0], total[3]]), total[1:3]
    got = to_y(jnp.where(outer, middle, ends).astype(BF16), lambda i: i ^ 1)
    total = jnp.where(outer, ends, middle) + got.astype(F32)
    got = to_y(jnp.where(y < 2, total[1], total[0]).astype(BF16), lambda i: 3 - i)
    total = jnp.where(y < 2, total[0], total[1]) + got.astype(F32)
    total = lax.psum_scatter(total.astype(BF16), "tensor", axis_index_groups=HIGH_PAIRS)
    return after(total, late).astype(F32)


def scatter_x(parts, x):
    width = parts.shape[1] // 2
    parts = parts.reshape(NX, -1, 2 * width)
    across, right, left = (pick(parts, (x + step) % NX, 0) for step in (2, 1, 3))
    gate_far = to_x(across[:, :width], 1)
    up_far = to_x(across[:, width:], -1)
    gate_right = to_x((right[:, :width].astype(F32) + gate_far.astype(F32)).astype(BF16), 1)
    up_left = to_x((left[:, width:].astype(F32) + up_far.astype(F32)).astype(BF16), -1)
    up_right = to_x(right[:, width:], 1)
    gate_left = to_x(left[:, :width], -1)
    own = pick(parts, x, 0).astype(F32)
    gate = own[:, :width] + gate_left.astype(F32) + gate_right.astype(F32)
    gate, up_left = lax.optimization_barrier((gate, up_left))
    up = own[:, width:] + up_right.astype(F32) + up_left.astype(F32)
    return gate, up


def scatter_z(total, z):
    total = total.reshape(2, 2, 2, total.shape[0] // NZ, -1)
    bits = ((z // 4) % 2, (z // 2) % 2, z % 2)
    for axis, bit in ((2, 1), (1, 2), (0, 4)):
        sent = pick(total, 1 - bits[axis], axis).astype(BF16)
        total = pick(total, bits[axis], axis) + to_z(sent, bit).astype(F32)
    return total, sent


def shards(tokens, masked, mask_vector, gate_weight, up_weight, cotangent):
    dp = lax.axis_index("dp")
    tensor = lax.axis_index("tensor")
    x, z = dp // NZ, dp % NZ
    y, high, core = tensor // 4, (tensor // 2) % 2, tensor % 2
    flag = masked[:, None] == 1
    mixed_in = jnp.where(flag, mask_vector[None, :], tokens)
    mixed_f = mixed_in.astype(F32)
    inverse = lax.rsqrt(jnp.mean(mixed_f * mixed_f, axis=-1, keepdims=True) + 1e-06)
    normed_full = mixed_f * inverse
    gathered = gather_rows(normed_full.astype(BF16), y, high, core)
    gate = jnp.dot(gathered, gate_weight, preferred_element_type=F32)
    up = jnp.dot(gathered, up_weight, preferred_element_type=F32)
    sig = jax.nn.sigmoid(gate)
    hidden = (gate * sig * up).astype(BF16)
    cot = cotangent.astype(F32)
    up_delta = (cot * gate * sig).astype(BF16)
    gate_delta = (cot * up * sig * (1.0 + gate * (1.0 - sig))).astype(BF16)
    contract_last = (((1,), (1,)), ((), ()))
    contract_first = (((0,), (0,)), ((), ()))
    deltas = jnp.concatenate([gate_delta, up_delta], axis=1)
    parts = lax.dot_general(gathered, deltas, contract_first, preferred_element_type=F32)
    gate_grad, up_grad = scatter_x(parts.astype(BF16), x)
    gate_grad, _ = scatter_z(gate_grad, z)
    up_grad, late = scatter_z(up_grad, z)
    first = lax.dot_general(gate_delta, gate_weight, contract_last, preferred_element_type=F32)
    second = lax.dot_general(up_delta, up_weight, contract_last, preferred_element_type=F32)
    normed_grad = scatter_rows((first + second).astype(BF16), late, y, core)
    inner = jnp.mean(normed_grad * normed_full, axis=-1, keepdims=True)
    token_grad = jnp.where(flag, 0.0, inverse * (normed_grad - normed_full * inner)).astype(BF16)
    return (hidden, token_grad, gate_grad, up_grad)


def solution(mesh):
    return jax.shard_map(
        shards,
        mesh=mesh,
        in_specs=(
            P(("dp", "tensor"), None),
            P(("dp", "tensor")),
            P(),
            P(None, "tensor"),
            P(None, "tensor"),
            P("dp", "tensor"),
        ),
        out_specs=(
            P("dp", "tensor"),
            P(("dp", "tensor"), None),
            P("dp", "tensor"),
            P("dp", "tensor"),
        ),
        check_vma=False,
    )
```

```python
import jax
import jax.numpy as jnp
from jax import lax
from jax.sharding import PartitionSpec as P

NX, NZ = 4, 8
NY, NH, NC = 4, 2, 2
F32, BF16 = jnp.float32, jnp.bfloat16


def pick(array, index, axis):
    return lax.dynamic_index_in_dim(array, index, axis, keepdims=False)


def choose(index, options):
    out = options[-1]
    for i in range(len(options) - 1):
        out = jnp.where(index == i, options[i], out)
    return out


def wait(array, early):
    rows, width = early.shape[0], array.shape[-1]
    early = jnp.tile(early, (1, -(-width // early.shape[1])))[:, :width]
    held = jnp.where(early == early, array.reshape(-1, rows, width), 0)
    return held.reshape(array.shape)


def move(array, axis_name, count, target):
    return lax.ppermute(array, axis_name, [(i, target(i)) for i in range(count)])


def to_core(array):
    return move(array, "tensor", 16, lambda t: t ^ 1)


def to_high(array):
    return move(array, "tensor", 16, lambda t: t ^ 2)


def to_y(array, step):
    return move(array, "tensor", 16, lambda t: (t + 4 * step) % 16)


def to_x(array, step):
    def target(i):
        d, t = i // 16, i % 16
        return (d + 8 * (step if t % 2 == 0 else -step)) % 32 * 16 + t

    return move(array, ("dp", "tensor"), 512, target)


def to_z(array, bit):
    return move(array, "dp", 32, lambda d: d ^ bit)


def gather_rows(normed, y, high, core):
    rows, depth = normed.shape
    other = to_high(normed)
    pair = jnp.where(high == 0, jnp.stack([normed, other]), jnp.stack([other, normed]))
    got = [to_y(pair, step) for step in (1, 2, 3)]
    ring = [pair, got[2], got[1], got[0]]
    quad = jnp.stack([choose(y, [ring[(i - j) % NY] for j in range(NY)]) for i in range(NY)])
    far = to_core(quad)
    both = jnp.where(core == 0, jnp.stack([quad, far], axis=2), jnp.stack([far, quad], axis=2))
    return both.reshape(16 * rows, depth)


def scatter_rows(share, y, high, core):
    rows = share.shape[0] // 16
    share = share.reshape(NY, NH, NC, rows, -1)
    got = to_core(pick(share, 1 - core, 2))
    total = pick(share, core, 2).astype(F32) + got.astype(F32)
    sent = total.astype(BF16)
    got = [to_y(pick(sent, (y + step) % NY, 0), step) for step in (1, 2, 3)]
    total = pick(total, y, 0)
    for part in got:
        total = total + part.astype(F32)
    return total


def scatter_high(total, late, high):
    got = wait(to_high(pick(total, 1 - high, 0).astype(BF16)), late)
    return pick(total, high, 0) + got.astype(F32)


def scatter_x(gathered, deltas, x, core):
    width = gathered.shape[1] // NX
    quarters = [gathered[:, i * width : (i + 1) * width] for i in range(NX)]

    def part(i):
        rows = choose(i, quarters)
        dims = (((0,), (0,)), ((), ()))
        return lax.dot_general(rows, deltas, dims, preferred_element_type=F32).astype(BF16)

    ahead = jnp.where(core == 0, 1, 3)
    far = to_x(part((x + 2) % NX), 1)
    joined = part((x + ahead) % NX).astype(F32) + far.astype(F32)
    joined = joined.astype(BF16)
    last = to_x(joined, 1)
    near = to_x(wait(part((x + 4 - ahead) % NX), joined[:16]), -1)
    return part(x).astype(F32) + near.astype(F32) + last.astype(F32)


def scatter_z(total, z, bit, axis):
    mine = (z // bit) % 2
    sent = pick(total, 1 - mine, axis).astype(BF16)
    return pick(total, mine, axis) + to_z(sent, bit).astype(F32)


def shards(tokens, masked, mask_vector, gate_weight, up_weight, cotangent):
    depth, width = gate_weight.shape
    dp = lax.axis_index("dp")
    tensor = lax.axis_index("tensor")
    x, z = dp // NZ, dp % NZ
    y, high, core = tensor // 4, (tensor // 2) % 2, tensor % 2
    flag = masked[:, None] == 1
    mixed_in = jnp.where(flag, mask_vector[None, :], tokens)
    mixed_f = mixed_in.astype(F32)
    inverse = lax.rsqrt(jnp.mean(mixed_f * mixed_f, axis=-1, keepdims=True) + 1e-06)
    normed_full = mixed_f * inverse
    gathered = gather_rows(normed_full.astype(BF16), y, high, core)
    gate = jnp.dot(gathered, gate_weight, preferred_element_type=F32)
    up = jnp.dot(gathered, up_weight, preferred_element_type=F32)
    sig = jax.nn.sigmoid(gate)
    hidden = (gate * sig * up).astype(BF16)
    cot = cotangent.astype(F32)
    up_delta = (cot * gate * sig).astype(BF16)
    gate_delta = (cot * up * sig * (1.0 + gate * (1.0 - sig))).astype(BF16)
    contract_last = (((1,), (1,)), ((), ()))
    deltas = jnp.concatenate([gate_delta, up_delta], axis=1)
    first = lax.dot_general(gate_delta, gate_weight, contract_last, preferred_element_type=F32)
    second = lax.dot_general(up_delta, up_weight, contract_last, preferred_element_type=F32)
    rows = scatter_rows((first + second).astype(BF16), y, high, core)
    total = scatter_x(gathered, deltas, x, core)
    normed_grad = scatter_high(rows, total[:16], high)
    total = total.reshape(2, 2, 2, depth // (NX * NZ), 2 * width)
    gate_grad = scatter_z(total[..., :width], z, 1, 2)
    up_grad = scatter_z(total[..., width:], z, 1, 2)
    gate_grad = scatter_z(gate_grad, z, 2, 1)
    up_grad = scatter_z(up_grad, z, 2, 1)
    gate_grad = scatter_z(gate_grad, z, 4, 0)
    up_grad = scatter_z(up_grad, z, 4, 0)
    inner = jnp.mean(normed_grad * normed_full, axis=-1, keepdims=True)
    token_grad = jnp.where(flag, 0.0, inverse * (normed_grad - normed_full * inner)).astype(BF16)
    return (hidden, token_grad, gate_grad, up_grad)


def solution(mesh):
    return jax.shard_map(
        shards,
        mesh=mesh,
        in_specs=(
            P(("dp", "tensor"), None),
            P(("dp", "tensor")),
            P(),
            P(None, "tensor"),
            P(None, "tensor"),
            P("dp", "tensor"),
        ),
        out_specs=(
            P("dp", "tensor"),
            P(("dp", "tensor"), None),
            P("dp", "tensor"),
            P("dp", "tensor"),
        ),
        check_vma=False,
    )
```

```python
import jax
import jax.numpy as jnp
from jax import lax
from jax.sharding import PartitionSpec as P

NX, NZ = 4, 8
NY, NH, NC = 4, 2, 2
F32, BF16 = jnp.float32, jnp.bfloat16


def pick(array, index, axis):
    return lax.dynamic_index_in_dim(array, index, axis, keepdims=False)


def choose(index, options):
    out = options[-1]
    for i in range(len(options) - 1):
        out = jnp.where(index == i, options[i], out)
    return out


def wait(array, row):
    width = array.shape[-1]
    row = jnp.tile(row, -(-width // row.shape[0]))[:width]
    return jnp.where(row == row, array, 0)


def move(array, axis_name, count, target):
    return lax.ppermute(array, axis_name, [(i, target(i)) for i in range(count)])


def to_core(array):
    return move(array, "tensor", 16, lambda t: t ^ 1)


def to_high(array):
    return move(array, "tensor", 16, lambda t: t ^ 2)


def to_y(array, step):
    return move(array, "tensor", 16, lambda t: (t + 4 * step) % 16)


def to_x(array, step):
    def target(i):
        d, t = i // 16, i % 16
        return (d + 8 * (step if t % 2 == 0 else -step)) % 32 * 16 + t

    return move(array, ("dp", "tensor"), 512, target)


def to_z(array, bit):
    return move(array, "dp", 32, lambda d: d ^ bit)


def gather_rows(normed, y, high, core):
    rows, depth = normed.shape
    other = to_high(normed)
    pair = jnp.where(high == 0, jnp.stack([normed, other]), jnp.stack([other, normed]))
    got = [to_y(pair, step) for step in (1, 2, 3)]
    ring = [pair, got[2], got[1], got[0]]
    quad = jnp.stack([choose(y, [ring[(i - j) % NY] for j in range(NY)]) for i in range(NY)])
    far = to_core(quad)
    both = jnp.where(core == 0, jnp.stack([quad, far], axis=2), jnp.stack([far, quad], axis=2))
    return both.reshape(16 * rows, depth)


def scatter_rows(share, y, high, core):
    rows = share.shape[0] // 16
    share = share.reshape(NY, NH, NC, rows, -1)
    got = to_core(pick(share, 1 - core, 2))
    total = pick(share, core, 2).astype(F32) + got.astype(F32)
    sent = total.astype(BF16)
    got = [to_y(pick(sent, (y + step) % NY, 0), step) for step in (1, 2, 3)]
    total = pick(total, y, 0)
    for part in got:
        total = total + part.astype(F32)
    return total, sent[0, 0, 0]


def scatter_high(total, late, high):
    got = wait(to_high(pick(total, 1 - high, 0).astype(BF16)), late)
    return pick(total, high, 0) + got.astype(F32)


def scatter_x(gate, up, early, x, core):
    def part(i):
        return jnp.stack([pick(gate, i % NX, 0), pick(up, i % NX, 0)])

    ahead = jnp.where(core == 0, 1, 3)
    far = to_x(part(x + 2), 1)
    near = to_x(wait(part(x + 4 - ahead), early), -1)
    joined = part(x + ahead).astype(F32) + far.astype(F32)
    last = to_x(joined.astype(BF16), 1)
    return part(x).astype(F32) + near.astype(F32) + last.astype(F32)


def scatter_z(total, z, bit, axis):
    mine = (z // bit) % 2
    sent = pick(total, 1 - mine, axis).astype(BF16)
    return pick(total, mine, axis) + to_z(sent, bit).astype(F32)


def shards(tokens, masked, mask_vector, gate_weight, up_weight, cotangent):
    depth, width = gate_weight.shape
    dp = lax.axis_index("dp")
    tensor = lax.axis_index("tensor")
    x, z = dp // NZ, dp % NZ
    y, high, core = tensor // 4, (tensor // 2) % 2, tensor % 2
    flag = masked[:, None] == 1
    mixed_in = jnp.where(flag, mask_vector[None, :], tokens)
    mixed_f = mixed_in.astype(F32)
    inverse = lax.rsqrt(jnp.mean(mixed_f * mixed_f, axis=-1, keepdims=True) + 1e-06)
    normed_full = mixed_f * inverse
    gathered = gather_rows(normed_full.astype(BF16), y, high, core)
    gate = jnp.dot(gathered, gate_weight, preferred_element_type=F32)
    up = jnp.dot(gathered, up_weight, preferred_element_type=F32)
    sig = jax.nn.sigmoid(gate)
    hidden = (gate * sig * up).astype(BF16)
    cot = cotangent.astype(F32)
    up_delta = (cot * gate * sig).astype(BF16)
    gate_delta = (cot * up * sig * (1.0 + gate * (1.0 - sig))).astype(BF16)
    contract_last = (((1,), (1,)), ((), ()))
    contract_first = (((0,), (0,)), ((), ()))
    first = lax.dot_general(gathered, gate_delta, contract_first, preferred_element_type=F32)
    second = lax.dot_general(gathered, up_delta, contract_first, preferred_element_type=F32)
    gate_parts = first.astype(BF16).reshape(NX, depth // NX, width)
    up_parts = second.astype(BF16).reshape(NX, depth // NX, width)
    first = lax.dot_general(gate_delta, gate_weight, contract_last, preferred_element_type=F32)
    second = lax.dot_general(up_delta, up_weight, contract_last, preferred_element_type=F32)
    rows, early = scatter_rows((first + second).astype(BF16), y, high, core)
    total = scatter_x(gate_parts, up_parts, early, x, core)
    normed_grad = scatter_high(rows, total[0, 0], high)
    total = total.reshape(2, 2, 2, 2, depth // (NX * NZ), width)
    gate_grad, up_grad = scatter_z(total[0], z, 1, 2), scatter_z(total[1], z, 1, 2)
    gate_grad, up_grad = scatter_z(gate_grad, z, 2, 1), scatter_z(up_grad, z, 2, 1)
    gate_grad, up_grad = scatter_z(gate_grad, z, 4, 0), scatter_z(up_grad, z, 4, 0)
    inner = jnp.mean(normed_grad * normed_full, axis=-1, keepdims=True)
    token_grad = jnp.where(flag, 0.0, inverse * (normed_grad - normed_full * inner)).astype(BF16)
    return (hidden, token_grad, gate_grad, up_grad)


def solution(mesh):
    return jax.shard_map(
        shards,
        mesh=mesh,
        in_specs=(
            P(("dp", "tensor"), None),
            P(("dp", "tensor")),
            P(),
            P(None, "tensor"),
            P(None, "tensor"),
            P("dp", "tensor"),
        ),
        out_specs=(
            P("dp", "tensor"),
            P(("dp", "tensor"), None),
            P("dp", "tensor"),
            P("dp", "tensor"),
        ),
        check_vma=False,
    )
```

```python
import jax
import jax.numpy as jnp
from jax import lax
from jax.sharding import PartitionSpec as P

NX, NZ = 4, 8
NY, NH, NC = 4, 2, 2
F32, BF16 = jnp.float32, jnp.bfloat16


def pick(array, index, axis):
    return lax.dynamic_index_in_dim(array, index, axis, keepdims=False)


def wait(array, row):
    width = array.shape[-1]
    row = jnp.tile(row, -(-width // row.shape[0]))[:width]
    return jnp.where(row == row, array, 0)


def move(array, axis_name, count, target):
    return lax.ppermute(array, axis_name, [(i, target(i)) for i in range(count)])


def to_core(array):
    return move(array, "tensor", 16, lambda t: t ^ 1)


def to_high(array):
    return move(array, "tensor", 16, lambda t: t ^ 2)


def to_y(array, step):
    return move(array, "tensor", 16, lambda t: (t + 4 * step) % 16)


def to_x(array, step):
    def target(i):
        d, t = i // 16, i % 16
        return (d + 8 * (step if t % 2 == 0 else -step)) % 32 * 16 + t

    return move(array, ("dp", "tensor"), 512, target)


def to_z(array, bit):
    return move(array, "dp", 32, lambda d: d ^ bit)


def gather_rows(normed, y, high, core):
    rows, depth = normed.shape
    other = to_high(normed)
    pair = jnp.where(high == 0, jnp.stack([normed, other]), jnp.stack([other, normed]))
    got = [to_y(pair, step) for step in (1, 2, 3)]
    ring = jnp.stack([pair, got[2], got[1], got[0]])
    quad = lax.dynamic_slice_in_dim(jnp.concatenate([ring, ring]), (NY - y) % NY, NY, 0)
    far = to_core(quad)
    both = jnp.where(core == 0, jnp.stack([quad, far], axis=2), jnp.stack([far, quad], axis=2))
    return both.reshape(16 * rows, depth)


def scatter_rows(share, y, high, core):
    rows = share.shape[0] // 16
    share = share.reshape(NY, NH, NC, rows, -1)
    got = to_core(pick(share, 1 - core, 2))
    total = pick(share, core, 2).astype(F32) + got.astype(F32)
    sent = total.astype(BF16)
    got = [to_y(pick(sent, (y + step) % NY, 0), step) for step in (1, 2, 3)]
    total = pick(total, y, 0)
    for part in got:
        total = total + part.astype(F32)
    return total, sent[0, 0, 0]


def scatter_high(total, late, high):
    got = wait(to_high(pick(total, 1 - high, 0).astype(BF16)), late)
    return pick(total, high, 0) + got.astype(F32)


def scatter_x(gate, up, early, x, core):
    def part(i):
        return jnp.stack([pick(gate, i % NX, 0), pick(up, i % NX, 0)])

    ahead = jnp.where(core == 0, 1, 3)
    far = to_x(part(x + 2), 1)
    near = to_x(wait(part(x + 4 - ahead), early), -1)
    joined = part(x + ahead).astype(F32) + far.astype(F32)
    last = to_x(joined.astype(BF16), 1)
    return part(x), near, last


def scatter_z(terms, z, bit, axis):
    mine = (z // bit) % 2

    def total(index):
        return sum(pick(term, index, axis).astype(F32) for term in terms)

    sent = total(1 - mine).astype(BF16)
    return total(mine) + to_z(sent, bit).astype(F32), sent


def shards(tokens, masked, mask_vector, gate_weight, up_weight, cotangent):
    depth, width = gate_weight.shape
    dp = lax.axis_index("dp")
    tensor = lax.axis_index("tensor")
    x, z = dp // NZ, dp % NZ
    y, high, core = tensor // 4, (tensor // 2) % 2, tensor % 2
    flag = masked[:, None] == 1
    mixed_in = jnp.where(flag, mask_vector[None, :], tokens)
    mixed_f = mixed_in.astype(F32)
    inverse = lax.rsqrt(jnp.mean(mixed_f * mixed_f, axis=-1, keepdims=True) + 1e-06)
    normed_full = mixed_f * inverse
    gathered = gather_rows(normed_full.astype(BF16), y, high, core)
    gate = jnp.dot(gathered, gate_weight, preferred_element_type=F32)
    up = jnp.dot(gathered, up_weight, preferred_element_type=F32)
    sig = jax.nn.sigmoid(gate)
    hidden = (gate * sig * up).astype(BF16)
    cot = cotangent.astype(F32)
    up_delta = (cot * gate * sig).astype(BF16)
    gate_delta = (cot * up * sig * (1.0 + gate * (1.0 - sig))).astype(BF16)
    contract_last = (((1,), (1,)), ((), ()))
    contract_first = (((0,), (0,)), ((), ()))
    first = lax.dot_general(gathered, gate_delta, contract_first, preferred_element_type=F32)
    second = lax.dot_general(gathered, up_delta, contract_first, preferred_element_type=F32)
    gate_parts = first.astype(BF16).reshape(NX, depth // NX, width)
    up_parts = second.astype(BF16).reshape(NX, depth // NX, width)
    first = lax.dot_general(gate_delta, gate_weight, contract_last, preferred_element_type=F32)
    second = lax.dot_general(up_delta, up_weight, contract_last, preferred_element_type=F32)
    rows, early = scatter_rows((first + second).astype(BF16), y, high, core)
    terms = scatter_x(gate_parts, up_parts, early, x, core)
    terms = [term.reshape(2, 2, 2, 2, depth // (NX * NZ), width) for term in terms]
    gate_grad, _ = scatter_z([term[0] for term in terms], z, 1, 2)
    up_grad, late = scatter_z([term[1] for term in terms], z, 1, 2)
    normed_grad = scatter_high(rows, late[0, 0, 0], high)
    gate_grad, up_grad = scatter_z([gate_grad], z, 2, 1)[0], scatter_z([up_grad], z, 2, 1)[0]
    gate_grad, up_grad = scatter_z([gate_grad], z, 4, 0)[0], scatter_z([up_grad], z, 4, 0)[0]
    inner = jnp.mean(normed_grad * normed_full, axis=-1, keepdims=True)
    token_grad = jnp.where(flag, 0.0, inverse * (normed_grad - normed_full * inner)).astype(BF16)
    return (hidden, token_grad, gate_grad, up_grad)


def solution(mesh):
    return jax.shard_map(
        shards,
        mesh=mesh,
        in_specs=(
            P(("dp", "tensor"), None),
            P(("dp", "tensor")),
            P(),
            P(None, "tensor"),
            P(None, "tensor"),
            P("dp", "tensor"),
        ),
        out_specs=(
            P("dp", "tensor"),
            P(("dp", "tensor"), None),
            P("dp", "tensor"),
            P("dp", "tensor"),
        ),
        check_vma=False,
    )
```

```python
import jax
import jax.numpy as jnp
from jax import lax
from jax.sharding import PartitionSpec as P

NX, NZ = 4, 8
NY, NH, NC = 4, 2, 2
F32, BF16 = jnp.float32, jnp.bfloat16


def pick(array, index, axis):
    return lax.dynamic_index_in_dim(array, index, axis, keepdims=False)


def wait(array, row):
    width = array.shape[-1]
    row = jnp.tile(row, -(-width // row.shape[0]))[:width]
    return jnp.where(row == row, array, 0)


def move(array, axis_name, count, target):
    return lax.ppermute(array, axis_name, [(i, target(i)) for i in range(count)])


def to_core(array):
    return move(array, "tensor", 16, lambda t: t ^ 1)


def to_high(array):
    return move(array, "tensor", 16, lambda t: t ^ 2)


def to_y(array, step):
    return move(array, "tensor", 16, lambda t: (t + 4 * step) % 16)


def to_x(array, step):
    def target(i):
        d, t = i // 16, i % 16
        return (d + 8 * (step if t % 2 == 0 else -step)) % 32 * 16 + t

    return move(array, ("dp", "tensor"), 512, target)


def to_z(array, bit):
    return move(array, "dp", 32, lambda d: d ^ bit)


def gather_rows(normed, y, high, core):
    rows, depth = normed.shape
    other = to_high(normed)
    pair = jnp.where(high == 0, jnp.stack([normed, other]), jnp.stack([other, normed]))
    got = [to_y(pair, step) for step in (1, 2, 3)]
    ring = jnp.stack([pair, got[2], got[1], got[0]])
    quad = lax.dynamic_slice_in_dim(jnp.concatenate([ring, ring]), (NY - y) % NY, NY, 0)
    far = to_core(quad)
    both = jnp.where(core == 0, jnp.stack([quad, far], axis=2), jnp.stack([far, quad], axis=2))
    return both.reshape(16 * rows, depth)


def scatter_rows(share, y, high, core):
    rows = share.shape[0] // 16
    share = share.reshape(NY, NH, NC, rows, -1)
    got = to_core(pick(share, 1 - core, 2))
    total = pick(share, core, 2).astype(F32) + got.astype(F32)
    sent = total.astype(BF16)
    got = [to_y(pick(sent, (y + step) % NY, 0), step) for step in (1, 2, 3)]
    total = pick(total, y, 0)
    for part in got:
        total = total + part.astype(F32)
    return total, sent[0, 0, 0]


def scatter_high(total, late, high):
    got = wait(to_high(pick(total, 1 - high, 0).astype(BF16)), late)
    return pick(total, high, 0) + got.astype(F32)


def scatter_x(gate, up, early, x, core):
    def part(i):
        return jnp.stack([pick(gate, i % NX, 0), pick(up, i % NX, 0)])

    ahead = jnp.where(core == 0, 1, 3)
    far = to_x(part(x + 2), 1)
    near = to_x(wait(part(x + 4 - ahead), early), -1)
    joined = part(x + ahead).astype(F32) + far.astype(F32)
    last = to_x(joined.astype(BF16), 1)
    return part(x), near, last


def scatter_z(terms, z, bit, axis):
    mine = (z // bit) % 2

    def total(index):
        return sum(pick(term, index, axis).astype(F32) for term in terms)

    sent = total(1 - mine).astype(BF16)
    return total(mine) + to_z(sent, bit).astype(F32), sent


def shards(tokens, masked, mask_vector, gate_weight, up_weight, cotangent):
    depth, width = gate_weight.shape
    dp = lax.axis_index("dp")
    tensor = lax.axis_index("tensor")
    x, z = dp // NZ, dp % NZ
    y, high, core = tensor // 4, (tensor // 2) % 2, tensor % 2
    flag = masked[:, None] == 1
    mixed_in = jnp.where(flag, mask_vector[None, :], tokens)
    mixed_f = mixed_in.astype(F32)
    inverse = lax.rsqrt(jnp.mean(mixed_f * mixed_f, axis=-1, keepdims=True) + 1e-06)
    normed_full = mixed_f * inverse
    gathered = gather_rows(normed_full.astype(BF16), y, high, core)
    gate = jnp.dot(gathered, gate_weight, preferred_element_type=F32)
    up = jnp.dot(gathered, up_weight, preferred_element_type=F32)
    sig = jax.nn.sigmoid(gate)
    hidden = (gate * sig * up).astype(BF16)
    cot = cotangent.astype(F32)
    up_delta = (cot * gate * sig).astype(BF16)
    gate_delta = (cot * up * sig * (1.0 + gate * (1.0 - sig))).astype(BF16)
    contract_last = (((1,), (1,)), ((), ()))
    contract_first = (((0,), (0,)), ((), ()))
    first = lax.dot_general(gathered, gate_delta, contract_first, preferred_element_type=F32)
    second = lax.dot_general(gathered, up_delta, contract_first, preferred_element_type=F32)
    gate_parts = first.astype(BF16).reshape(NX, depth // NX, width)
    up_parts = second.astype(BF16).reshape(NX, depth // NX, width)
    first = lax.dot_general(gate_delta, gate_weight, contract_last, preferred_element_type=F32)
    second = lax.dot_general(up_delta, up_weight, contract_last, preferred_element_type=F32)
    rows, early = scatter_rows((first + second).astype(BF16), y, high, core)
    terms = scatter_x(gate_parts, up_parts, early, x, core)
    terms = [term.reshape(2, 2, 2, 2, depth // (NX * NZ), width) for term in terms]
    total, late = scatter_z(terms, z, 1, 3)
    normed_grad = scatter_high(rows, late[0, 0, 0, 0], high)
    gate_grad, up_grad = total[0], total[1]
    gate_grad, up_grad = scatter_z([gate_grad], z, 2, 1)[0], scatter_z([up_grad], z, 2, 1)[0]
    gate_grad, up_grad = scatter_z([gate_grad], z, 4, 0)[0], scatter_z([up_grad], z, 4, 0)[0]
    inner = jnp.mean(normed_grad * normed_full, axis=-1, keepdims=True)
    token_grad = jnp.where(flag, 0.0, inverse * (normed_grad - normed_full * inner)).astype(BF16)
    return (hidden, token_grad, gate_grad, up_grad)


def solution(mesh):
    return jax.shard_map(
        shards,
        mesh=mesh,
        in_specs=(
            P(("dp", "tensor"), None),
            P(("dp", "tensor")),
            P(),
            P(None, "tensor"),
            P(None, "tensor"),
            P("dp", "tensor"),
        ),
        out_specs=(
            P("dp", "tensor"),
            P(("dp", "tensor"), None),
            P("dp", "tensor"),
            P("dp", "tensor"),
        ),
        check_vma=False,
    )
```

```python
import jax
import jax.numpy as jnp
from jax import lax
from jax.experimental import pallas as pl
from jax.experimental.pallas import tpu as pltpu
from jax.sharding import PartitionSpec as P

NX, NZ = 4, 8
NY, NH, NC = 4, 2, 2
F32, BF16 = jnp.float32, jnp.bfloat16


def pick(array, index, axis):
    return lax.dynamic_index_in_dim(array, index, axis, keepdims=False)


def wait(array, row):
    width = array.shape[-1]
    row = jnp.tile(row, -(-width // row.shape[0]))[:width]
    return jnp.where(row == row, array, 0)


def move(array, axis_name, count, target):
    return lax.ppermute(array, axis_name, [(i, target(i)) for i in range(count)])


def to_core(array):
    return move(array, "tensor", 16, lambda t: t ^ 1)


def to_high(array):
    return move(array, "tensor", 16, lambda t: t ^ 2)


def to_y(array, step):
    return move(array, "tensor", 16, lambda t: (t + 4 * step) % 16)


def to_x(array, step):
    def target(i):
        d, t = i // 16, i % 16
        return (d + 8 * (step if t % 2 == 0 else -step)) % 32 * 16 + t

    return move(array, ("dp", "tensor"), 512, target)


def to_z(array, bit):
    return move(array, "dp", 32, lambda d: d ^ bit)


def gather_rows(normed, y, high, core):
    rows, depth = normed.shape
    other = to_high(normed)
    pair = jnp.where(high == 0, jnp.stack([normed, other]), jnp.stack([other, normed]))
    got = [to_y(pair, step) for step in (1, 2, 3)]
    ring = jnp.stack([pair, got[2], got[1], got[0]])
    quad = lax.dynamic_slice_in_dim(jnp.concatenate([ring, ring]), (NY - y) % NY, NY, 0)
    far = to_core(quad)
    both = jnp.where(core == 0, jnp.stack([quad, far], axis=2), jnp.stack([far, quad], axis=2))
    return both.reshape(16 * rows, depth)


def scatter_rows(share, y, high, core):
    rows = share.shape[0] // 16
    share = share.reshape(NY, NH, NC, rows, -1)
    got = to_core(pick(share, 1 - core, 2))
    total = pick(share, core, 2).astype(F32) + got.astype(F32)
    sent = total.astype(BF16)
    got = [to_y(pick(sent, (y + step) % NY, 0), step) for step in (1, 2, 3)]
    total = pick(total, y, 0)
    for part in got:
        total = total + part.astype(F32)
    return total, sent[0, 0, 0]


def scatter_high(total, late, high):
    got = wait(to_high(pick(total, 1 - high, 0).astype(BF16)), late)
    return pick(total, high, 0) + got.astype(F32)


def scatter_x(gate, up, early, x, core):
    def part(i):
        return jnp.stack([pick(gate, i % NX, 0), pick(up, i % NX, 0)])

    ahead = jnp.where(core == 0, 1, 3)
    far = to_x(part(x + 2), 1)
    near = to_x(wait(part(x + 4 - ahead), early), -1)
    joined = part(x + ahead).astype(F32) + far.astype(F32)
    last = to_x(joined.astype(BF16), 1)
    return part(x), near, last


def scatter_z(terms, z, bit, axis):
    mine = (z // bit) % 2

    def total(index):
        return sum(pick(term, index, axis).astype(F32) for term in terms)

    sent = total(1 - mine).astype(BF16)
    return total(mine) + to_z(sent, bit).astype(F32), sent


def norm_kernel(masked_ref, tokens_ref, vector_ref, normed_ref):
    rows = tokens_ref.shape[0]
    index = lax.broadcasted_iota(jnp.int32, (rows, 1), 0)
    flag = jnp.zeros((rows, 1), jnp.int32)
    for i in range(rows):
        flag = jnp.where(index == i, masked_ref[i], flag)
    mixed = jnp.where(flag == 1, vector_ref[...].astype(F32), tokens_ref[...].astype(F32))
    inverse = lax.rsqrt(jnp.mean(mixed * mixed, axis=-1, keepdims=True) + 1e-06)
    normed_ref[...] = (mixed * inverse).astype(BF16)


def norm(masked, tokens, mask_vector):
    return pl.pallas_call(
        norm_kernel,
        out_shape=jax.ShapeDtypeStruct(tokens.shape, BF16),
        in_specs=[pl.BlockSpec(memory_space=pltpu.SMEM)] + [pl.BlockSpec(memory_space=pltpu.VMEM)] * 2,
        out_specs=pl.BlockSpec(memory_space=pltpu.VMEM),
        compiler_params=pltpu.CompilerParams(vmem_limit_bytes=4 * 2**20),
    )(masked, tokens, mask_vector[None, :])


def shards(tokens, masked, mask_vector, gate_weight, up_weight, cotangent):
    depth, width = gate_weight.shape
    dp = lax.axis_index("dp")
    tensor = lax.axis_index("tensor")
    x, z = dp // NZ, dp % NZ
    y, high, core = tensor // 4, (tensor // 2) % 2, tensor % 2
    flag = masked[:, None] == 1
    mixed_in = jnp.where(flag, mask_vector[None, :], tokens)
    mixed_f = mixed_in.astype(F32)
    inverse = lax.rsqrt(jnp.mean(mixed_f * mixed_f, axis=-1, keepdims=True) + 1e-06)
    normed_full = mixed_f * inverse
    gathered = gather_rows(norm(masked, tokens, mask_vector), y, high, core)
    gate = jnp.dot(gathered, gate_weight, preferred_element_type=F32)
    up = jnp.dot(gathered, up_weight, preferred_element_type=F32)
    sig = jax.nn.sigmoid(gate)
    hidden = (gate * sig * up).astype(BF16)
    cot = cotangent.astype(F32)
    up_delta = (cot * gate * sig).astype(BF16)
    gate_delta = (cot * up * sig * (1.0 + gate * (1.0 - sig))).astype(BF16)
    contract_last = (((1,), (1,)), ((), ()))
    contract_first = (((0,), (0,)), ((), ()))
    first = lax.dot_general(gathered, gate_delta, contract_first, preferred_element_type=F32)
    second = lax.dot_general(gathered, up_delta, contract_first, preferred_element_type=F32)
    gate_parts = first.astype(BF16).reshape(NX, depth // NX, width)
    up_parts = second.astype(BF16).reshape(NX, depth // NX, width)
    first = lax.dot_general(gate_delta, gate_weight, contract_last, preferred_element_type=F32)
    second = lax.dot_general(up_delta, up_weight, contract_last, preferred_element_type=F32)
    rows, early = scatter_rows((first + second).astype(BF16), y, high, core)
    terms = scatter_x(gate_parts, up_parts, early, x, core)
    terms = [term.reshape(2, 2, 2, 2, depth // (NX * NZ), width) for term in terms]
    gate_grad, _ = scatter_z([term[0] for term in terms], z, 1, 2)
    up_grad, late = scatter_z([term[1] for term in terms], z, 1, 2)
    normed_grad = scatter_high(rows, late[0, 0, 0], high)
    gate_grad, up_grad = scatter_z([gate_grad], z, 2, 1)[0], scatter_z([up_grad], z, 2, 1)[0]
    gate_grad, up_grad = scatter_z([gate_grad], z, 4, 0)[0], scatter_z([up_grad], z, 4, 0)[0]
    inner = jnp.mean(normed_grad * normed_full, axis=-1, keepdims=True)
    token_grad = jnp.where(flag, 0.0, inverse * (normed_grad - normed_full * inner)).astype(BF16)
    return (hidden, token_grad, gate_grad, up_grad)


def solution(mesh):
    return jax.shard_map(
        shards,
        mesh=mesh,
        in_specs=(
            P(("dp", "tensor"), None),
            P(("dp", "tensor")),
            P(),
            P(None, "tensor"),
            P(None, "tensor"),
            P("dp", "tensor"),
        ),
        out_specs=(
            P("dp", "tensor"),
            P(("dp", "tensor"), None),
            P("dp", "tensor"),
            P("dp", "tensor"),
        ),
        check_vma=False,
    )
```

```python
import jax
import jax.numpy as jnp
from jax import lax
from jax.sharding import PartitionSpec as P

NX, NZ = 4, 8
NY, NH, NC = 4, 2, 2
F32, BF16 = jnp.float32, jnp.bfloat16


def pick(array, index, axis):
    return lax.dynamic_index_in_dim(array, index, axis, keepdims=False)


def wait(array, row):
    width = array.shape[-1]
    row = jnp.tile(row, -(-width // row.shape[0]))[:width]
    return jnp.where(row == row, array, 0)


def move(array, axis_name, count, target):
    return lax.ppermute(array, axis_name, [(i, target(i)) for i in range(count)])


def to_core(array):
    return move(array, "tensor", 16, lambda t: t ^ 1)


def to_high(array):
    return move(array, "tensor", 16, lambda t: t ^ 2)


def to_y(array, step):
    return move(array, "tensor", 16, lambda t: (t + 4 * step) % 16)


def to_x(array, step):
    def target(i):
        d, t = i // 16, i % 16
        return (d + 8 * (step if t % 2 == 0 else -step)) % 32 * 16 + t

    return move(array, ("dp", "tensor"), 512, target)


def to_z(array, bit):
    return move(array, "dp", 32, lambda d: d ^ bit)


def gather_rows(normed, y, high, core):
    rows, depth = normed.shape
    other = to_high(normed)
    pair = jnp.where(high == 0, jnp.stack([normed, other]), jnp.stack([other, normed]))
    got = [to_y(pair, step) for step in (1, 2, 3)]
    ring = jnp.stack([pair, got[2], got[1], got[0]])
    quad = lax.dynamic_slice_in_dim(jnp.concatenate([ring, ring]), (NY - y) % NY, NY, 0)
    far = to_core(quad)
    both = jnp.where(core == 0, jnp.stack([quad, far], axis=2), jnp.stack([far, quad], axis=2))
    return both.reshape(16 * rows, depth)


def scatter_rows(share, y, high, core):
    rows = share.shape[0] // 16
    share = share.reshape(NY, NH, NC, rows, -1)
    got = to_core(pick(share, 1 - core, 2))
    total = pick(share, core, 2).astype(F32) + got.astype(F32)
    sent = total.astype(BF16)
    got = [to_y(pick(sent, (y + step) % NY, 0), step) for step in (1, 2, 3)]
    total = pick(total, y, 0)
    for part in got:
        total = total + part.astype(F32)
    return total, sent[0, 0, 0]


def scatter_high(total, late, high):
    got = wait(to_high(pick(total, 1 - high, 0).astype(BF16)), late)
    return pick(total, high, 0) + got.astype(F32)


def scatter_x(gate, up, early, x, core):
    def part(i):
        return jnp.stack([pick(gate, i % NX, 0), pick(up, i % NX, 0)])

    ahead = jnp.where(core == 0, 1, 3)
    far = to_x(part(x + 2), 1)
    near = to_x(wait(part(x + 4 - ahead), early), -1)
    joined = part(x + ahead).astype(F32) + far.astype(F32)
    last = to_x(joined.astype(BF16), 1)
    return part(x), near, last


def scatter_z(terms, z, bit, axis):
    mine = (z // bit) % 2

    def total(index):
        return sum(pick(term, index, axis).astype(F32) for term in terms)

    sent = total(1 - mine).astype(BF16)
    return total(mine) + to_z(sent, bit).astype(F32), sent


def shards(tokens, masked, mask_vector, gate_weight, up_weight, cotangent):
    depth, width = gate_weight.shape
    dp = lax.axis_index("dp")
    tensor = lax.axis_index("tensor")
    x, z = dp // NZ, dp % NZ
    y, high, core = tensor // 4, (tensor // 2) % 2, tensor % 2
    flag = masked[:, None] == 1
    mixed_in = jnp.where(flag, mask_vector[None, :], tokens)
    mixed_f = mixed_in.astype(F32)
    inverse = lax.rsqrt(jnp.mean(mixed_f * mixed_f, axis=-1, keepdims=True) + 1e-06)
    normed_full = mixed_f * inverse
    gathered = gather_rows(normed_full.astype(BF16), y, high, core)
    gate = jnp.dot(gathered, gate_weight, preferred_element_type=F32)
    up = jnp.dot(gathered, up_weight, preferred_element_type=F32)
    sig = jax.nn.sigmoid(gate)
    hidden = (gate * sig * up).astype(BF16)
    cot = cotangent.astype(F32)
    up_delta = (cot * gate * sig).astype(BF16)
    gate_delta = (cot * up * sig * (1.0 + gate * (1.0 - sig))).astype(BF16)
    contract_last = (((1,), (1,)), ((), ()))
    contract_first = (((0,), (0,)), ((), ()))
    first = lax.dot_general(gathered, gate_delta, contract_first, preferred_element_type=F32)
    second = lax.dot_general(gathered, up_delta, contract_first, preferred_element_type=F32)
    gate_parts = first.astype(BF16).reshape(NX, depth // NX, width)
    up_parts = second.astype(BF16).reshape(NX, depth // NX, width)
    first = lax.dot_general(gate_delta, gate_weight, contract_last, preferred_element_type=F32)
    second = lax.dot_general(up_delta, up_weight, contract_last, preferred_element_type=F32)
    rows, early = scatter_rows((first + second).astype(BF16), y, high, core)
    terms = scatter_x(gate_parts, up_parts, early, x, core)
    terms = [term.reshape(2, 2, 2, 2, depth // (NX * NZ), width) for term in terms]
    gate_grad, _ = scatter_z([term[0] for term in terms], z, 1, 2)
    up_grad, _ = scatter_z([term[1] for term in terms], z, 1, 2)
    normed_grad = scatter_high(rows, terms[2][0, 0, 0, 0, 0], high)
    gate_grad, up_grad = scatter_z([gate_grad], z, 2, 1)[0], scatter_z([up_grad], z, 2, 1)[0]
    gate_grad, up_grad = scatter_z([gate_grad], z, 4, 0)[0], scatter_z([up_grad], z, 4, 0)[0]
    inner = jnp.mean(normed_grad * normed_full, axis=-1, keepdims=True)
    token_grad = jnp.where(flag, 0.0, inverse * (normed_grad - normed_full * inner)).astype(BF16)
    return (hidden, token_grad, gate_grad, up_grad)


def solution(mesh):
    return jax.shard_map(
        shards,
        mesh=mesh,
        in_specs=(
            P(("dp", "tensor"), None),
            P(("dp", "tensor")),
            P(),
            P(None, "tensor"),
            P(None, "tensor"),
            P("dp", "tensor"),
        ),
        out_specs=(
            P("dp", "tensor"),
            P(("dp", "tensor"), None),
            P("dp", "tensor"),
            P("dp", "tensor"),
        ),
        check_vma=False,
    )
```
